32 devices in a mesh: ctx: 4 (over y, x), shard: 4 (over z), replica: 2 (over core).
Axes of the slice: x: 2, y: 2, z: 4, core: 2. Of those that a mesh axis runs over, the one named last changes fastest.
Arguments:
- tokens: bfloat16 [8, 1024, 896], P(('shard', 'replica'), 'ctx'), may hold values from -6 to 6
- block_order: int32 [8, 8], P(('shard', 'replica')), may hold values from 0 to 7, as said below
- w_qkv: bfloat16 [896, 1152], P(('ctx', 'shard')), may hold values from -0.1875 to 0.1875
- qkv_bias: bfloat16 [1152], P(('ctx', 'shard')), may hold values from -3 to 3
- w_out: bfloat16 [896, 896], P(('ctx', 'shard')), may hold values from -1 to 1
- norm_gains: bfloat16 [2, 896], P(None, ('ctx', 'shard')), may hold values from 0.25 to 1.75
- w_gate: bfloat16 [896, 4864], P(('ctx', 'shard')), may hold values from -0.1875 to 0.1875
- w_up: bfloat16 [896, 4864], P(('ctx', 'shard')), may hold values from -0.1875 to 0.1875
- w_down: bfloat16 [4864, 896], P(('ctx', 'shard')), may hold values from -0.078125 to 0.078125
- cotangent: bfloat16 [8, 1024, 896], P(('shard', 'replica'), 'ctx'), may hold values from -6 to 6
Outputs:
- block_out: bfloat16 [8, 1024, 896], P(('shard', 'replica'), 'ctx')
- input_grad: float32 [8, 1024, 896], P(('shard', 'replica'), 'ctx')
- grad_qkv: float32 [896, 1152], P(('ctx', 'shard'))
- grad_bias: float32 [1152], P(('ctx', 'shard'))
- grad_out: float32 [896, 896], P(('ctx', 'shard'))
- grad_gains: float32 [2, 896], P(None, ('ctx', 'shard'))
- grad_gate: float32 [896, 4864], P(('ctx', 'shard'))
- grad_up: float32 [896, 4864], P(('ctx', 'shard'))
- grad_down: float32 [4864, 896], P(('ctx', 'shard'))
The draws below stay inside these ranges and needn't reach their ends.
Inputs may be any that keep to these rules, and one draw needn't show every extreme that they name: `block_order`: each row lists the 8 block numbers of one sequence, each once, and entries 2 k and 2 k + 1 sum to 7.
All inputs are finite; a program needn't handle non-finite values.
Results may differ from the reference program's by a relative error of at most 0.015.
Values may be sent and summed in bfloat16 or wider, within the bound.
A program may use at most 256 MiB of HBM per device.

```python
import math
import jax
import jax.numpy as jnp
from jax import lax

D = 896
Q_HEADS = 14
KV_HEADS = 2
HEAD_DIM = 64
FF = 4864
SEQ_LEN = 1024
SEQS = 8
N_CTX = 4


def pair_order(key):
    first_key, second_key = jax.random.split(key)
    pair_index = jax.random.permutation(first_key, N_CTX)
    flip_bits = jax.random.randint(second_key, (N_CTX,), 0, 2)
    leading = jnp.where(flip_bits == 1, 2 * N_CTX - 1 - pair_index, pair_index)
    return jnp.stack([leading, 2 * N_CTX - 1 - leading], axis=1).reshape(2 * N_CTX).astype(jnp.int32)


def draw_block_order(key, part):
    key = jax.random.fold_in(key, 11)
    return jax.vmap(pair_order)(jax.random.split(key, SEQS))


def levels(own_key, shape, shards, smallest, high):
    factor_of, own = 1.0, jax.random.fold_in(own_key, 6)
    for axis_at, blocks in shards:
        draws = jnp.exp(jax.random.uniform(jax.random.fold_in(own, axis_at), (blocks,), jnp.float32, smallest / len(shards), high / len(shards)))
        factor_of = factor_of * jnp.repeat(draws, shape[axis_at] // blocks).reshape([-1 if axis == axis_at else 1 for axis in range(len(shape))])
    return factor_of


def bell_draw(stream_key, extent, deviation, bound, pieces=(), kind=jnp.bfloat16):
    drawn = deviation * jax.random.normal(stream_key, extent, jnp.float32)
    if pieces:
        drawn = drawn * levels(stream_key, extent, pieces, -0.22, 0.18)
    return jnp.clip(drawn, -bound, bound).astype(kind)


def setup_inputs(seed: int = 0) -> dict:
    streams_of = jax.random.split(jax.random.key(seed), 11)
    tokens = bell_draw(streams_of[0], (SEQS, SEQ_LEN, D), 1.0, 6.0, ((0, 8), (1, 4)))
    block_order = draw_block_order(jax.random.fold_in(streams_of[10], 71), 0)
    w_qkv = bell_draw(streams_of[2], (D, D + 2 * KV_HEADS * HEAD_DIM), D ** -0.5, 0.1875, ((0, 16),))
    qkv_bias = bell_draw(streams_of[3], (D + 2 * KV_HEADS * HEAD_DIM,), 0.5, 3.0, ((0, 16),))
    w_out = bell_draw(streams_of[4], (D, D), (D // 32) ** -0.5, 1.0, ((0, 16),))
    norm_gains = jnp.clip(1.0 + 0.15 * jax.random.normal(streams_of[5], (2, D), jnp.float32), 0.25, 1.75).astype(jnp.bfloat16)
    w_gate = bell_draw(streams_of[6], (D, FF), D ** -0.5, 0.1875, ((0, 16),))
    w_up = bell_draw(streams_of[7], (D, FF), D ** -0.5, 0.1875, ((0, 16),))
    w_down = bell_draw(streams_of[8], (FF, D), FF ** -0.5, 0.078125, ((0, 16),))
    cotangent = bell_draw(streams_of[9], (SEQS, SEQ_LEN, D), 1.0, 6.0, ((0, 8), (1, 4)))
    return dict(tokens=tokens, block_order=block_order, w_qkv=w_qkv, qkv_bias=qkv_bias, w_out=w_out, norm_gains=norm_gains, w_gate=w_gate, w_up=w_up, w_down=w_down, cotangent=cotangent)


epsilon = 1e-06
rope_base = 1000000.0
score_scale = 0.125
masked_value = -1e+30

@jax.custom_vjp
def low(v):
    return lax.optimization_barrier(v.astype(jnp.bfloat16)).astype(jnp.float32)

@jax.custom_vjp
def low_back(v):
    return v

def low_keep(v):
    return (low(v), None)

def low_pass(kept, grad):
    return (grad,)

def back_keep(v):
    return (v, None)

def back_low(kept, grad):
    return (low(grad),)
low.defvjp(low_keep, low_pass)
low_back.defvjp(back_keep, back_low)

def rope_tables(positions):
    half_dim = HEAD_DIM // 2
    inverse = rope_base ** (-(jnp.arange(half_dim, dtype=jnp.float32) * 2.0) / HEAD_DIM)
    angles = positions.astype(jnp.float32)[..., None] * inverse
    angles = jnp.concatenate([angles, angles], axis=-1)
    return (jnp.cos(angles), jnp.sin(angles))

def rotate(values, cosine, sine):
    half_dim = values.shape[-1] // 2
    turned = jnp.concatenate([-values[..., half_dim:], values[..., :half_dim]], axis=-1)
    return values * cosine + turned * sine

def rms_norm(values, gain):
    return values * lax.rsqrt(lax.optimization_barrier(jnp.mean(values * values, axis=-1, keepdims=True)) + epsilon) * gain

def block_layer(params, inputs, positions):
    w_qkv, qkv_bias, w_out, norm_gains, w_gate, w_up, w_down = params
    highest = lax.Precision.HIGHEST
    groups, seq_len, model_width = inputs.shape
    kv_width = KV_HEADS * HEAD_DIM
    repeats = Q_HEADS // KV_HEADS
    normed_one = low(rms_norm(inputs, norm_gains[0]))
    projected = low_back(jnp.einsum('gld,de->gle', normed_one, w_qkv, precision=highest) + qkv_bias)
    cosine, sine = rope_tables(positions)
    queries = low(rotate(projected[..., :model_width].reshape(groups, seq_len, KV_HEADS, repeats, HEAD_DIM), cosine[:, :, None, None, :], sine[:, :, None, None, :]))
    key_rows = low(rotate(projected[..., model_width:model_width + kv_width].reshape(groups, seq_len, KV_HEADS, HEAD_DIM), cosine[:, :, None, :], sine[:, :, None, :]))
    value_rows = low(projected[..., model_width + kv_width:].reshape(groups, seq_len, KV_HEADS, HEAD_DIM))
    scores = low_back(jnp.einsum('gqhrd,gkhd->ghrqk', queries, key_rows, precision=highest) * score_scale)
    allowed = positions[:, None, None, :, None] >= positions[:, None, None, None, :]
    scores = jnp.where(allowed, scores, masked_value)
    attn_probs = low(jax.nn.softmax(scores, axis=-1))
    attended = jnp.einsum('ghrqk,gkhd->gqhrd', attn_probs, value_rows, precision=highest)
    attended = low(low_back(attended.reshape(groups, seq_len, model_width)))
    middle = inputs + low_back(jnp.einsum('gld,de->gle', attended, w_out, precision=highest))
    normed_two = low(rms_norm(middle, norm_gains[1]))
    gate_pre = low_back(jnp.einsum('gld,df->glf', normed_two, w_gate, precision=highest))
    up_pre = low_back(jnp.einsum('gld,df->glf', normed_two, w_up, precision=highest))
    act_rows = low(jax.nn.silu(gate_pre) * up_pre)
    return middle + low_back(jnp.einsum('glf,fd->gld', act_rows, w_down, precision=highest))

def reference(tokens, block_order, w_qkv, qkv_bias, w_out, norm_gains, w_gate, w_up, w_down, cotangent):
    block_len = SEQ_LEN // (2 * N_CTX)
    slots = jnp.arange(SEQ_LEN, dtype=jnp.int32)
    positions = (block_order[:, slots // block_len] * block_len + slots % block_len).astype(jnp.int32)
    params = (w_qkv.astype(jnp.float32), qkv_bias.astype(jnp.float32), w_out.astype(jnp.float32), norm_gains.astype(jnp.float32), w_gate.astype(jnp.float32), w_up.astype(jnp.float32), w_down.astype(jnp.float32))
    inputs = tokens.astype(jnp.float32)
    group_size = math.gcd(SEQS, 2)
    steps_count = SEQS // group_size
    checked = jax.checkpoint(block_layer)

    def whole_batch(weights, batch):
        batched = batch.reshape(steps_count, group_size, SEQ_LEN, D)
        placed = positions.reshape(steps_count, group_size, SEQ_LEN)

        def scan_step(carry, packed):
            return (carry, checked(weights, packed[0], packed[1]))
        carry_out, outputs = lax.scan(scan_step, jnp.zeros((), jnp.float32), (batched, placed))
        return outputs.reshape(SEQS, SEQ_LEN, D)
    block_out, pull_back = jax.vjp(whole_batch, params, inputs)
    param_grads, input_grad = pull_back(cotangent.astype(jnp.float32))
    return (block_out.astype(jnp.bfloat16), input_grad, param_grads[0], param_grads[1], param_grads[2], param_grads[3], param_grads[4], param_grads[5], param_grads[6])
```

```python
import jax
import jax.numpy as jnp
from jax import lax
from jax.sharding import PartitionSpec as P

Q_HEADS = 14
KV_HEADS = 2
HEAD_DIM = 64
SEQ_LEN = 1024


epsilon = 1e-06
rope_base = 1000000.0
score_scale = 0.125
masked_value = -1e30


def rope_tables(positions):
    half_dim = HEAD_DIM // 2
    inverse = rope_base ** (-(jnp.arange(half_dim, dtype=jnp.float32) * 2.0) / HEAD_DIM)
    angles = positions.astype(jnp.float32)[..., None] * inverse
    angles = jnp.concatenate([angles, angles], axis=-1)
    return (jnp.cos(angles), jnp.sin(angles))


def rotate(values, cosine, sine):
    half_dim = values.shape[-1] // 2
    turned = jnp.concatenate([-values[..., half_dim:], values[..., :half_dim]], axis=-1)
    return values * cosine + turned * sine


def rotate_back(grads, cosine, sine):
    half_dim = grads.shape[-1] // 2
    moved = grads * sine
    turned = jnp.concatenate([moved[..., half_dim:], -moved[..., :half_dim]], axis=-1)
    return grads * cosine + turned


def norm_back(inputs, inverse, gain, upstream):
    scaled = upstream * gain
    gain_term = jnp.sum(upstream * inputs * inverse, axis=0)
    input_term = inverse * scaled - inputs * inverse**3 * jnp.mean(
        scaled * inputs, axis=-1, keepdims=True
    )
    return (gain_term, input_term)


def masked_scores(queries, key_rows, pos_query, pos_key):
    scores = (
        jnp.einsum("qhrd,khd->hrqk", queries, key_rows, preferred_element_type=jnp.float32)
        * score_scale
    )
    allowed = pos_query[:, None] >= pos_key[None, :]
    return jnp.where(allowed, scores, masked_value)


def attend(packed):
    queries, key_rows, value_rows, pos_query, pos_key = packed
    scores = masked_scores(queries, key_rows, pos_query, pos_key)
    top_score = jnp.max(scores, axis=-1, keepdims=True)
    weights = jnp.exp(scores - top_score)
    totals = jnp.sum(weights, axis=-1, keepdims=True)
    attn_probs = (weights / totals).astype(jnp.bfloat16)
    mixed_out = jnp.einsum(
        "hrqk,khd->qhrd", attn_probs, value_rows, preferred_element_type=jnp.float32
    )
    return (mixed_out, top_score + jnp.log(totals))


def attend_back(packed):
    queries, key_rows, value_rows, upstream, logsum, pos_query, pos_key = packed
    scores = masked_scores(queries, key_rows, pos_query, pos_key)
    attn_probs = jnp.exp(scores - logsum)
    dprob = jnp.einsum("qhrd,khd->hrqk", upstream, value_rows, preferred_element_type=jnp.float32)
    row_dot = jnp.sum(attn_probs * dprob, axis=-1, keepdims=True)
    dscore = (attn_probs * (dprob - row_dot)).astype(jnp.bfloat16)
    grad_query = (
        jnp.einsum("hrqk,khd->qhrd", dscore, key_rows, preferred_element_type=jnp.float32)
        * score_scale
    )
    grad_key = (
        jnp.einsum("hrqk,qhrd->khd", dscore, queries, preferred_element_type=jnp.float32)
        * score_scale
    )
    grad_value = jnp.einsum(
        "hrqk,qhrd->khd",
        attn_probs.astype(jnp.bfloat16),
        upstream,
        preferred_element_type=jnp.float32,
    )
    return (grad_query, grad_key, grad_value)


def swap(values):
    return lax.ppermute(values, "replica", [(0, 1), (1, 0)])


def pair_sum(parts):
    mine = lax.axis_index("replica")
    kept = lax.dynamic_index_in_dim(parts, mine, 0, keepdims=False)
    sent = lax.dynamic_index_in_dim(parts, 1 - mine, 0, keepdims=False)
    return kept.astype(jnp.float32) + swap(sent.astype(jnp.bfloat16)).astype(jnp.float32)


def pair_join(values):
    first = lax.axis_index("replica") == 0
    other = swap(values)
    return jnp.stack([jnp.where(first, values, other), jnp.where(first, other, values)])


def scatter_rows(partial):
    rows, width = partial.shape
    replica_count = lax.axis_size("replica")
    ctx_count = lax.axis_size("ctx")
    parts = partial.reshape(ctx_count, replica_count, -1, width).transpose(1, 0, 2, 3)
    parts = pair_sum(parts).astype(jnp.bfloat16)
    return lax.psum_scatter(parts, "ctx", scatter_dimension=0, tiled=False)


def owner_sum(grad):
    rows, width = grad.shape
    replica_count = lax.axis_size("replica")
    parts = grad.reshape(rows, replica_count, -1).transpose(1, 0, 2)
    parts = pair_sum(parts).astype(jnp.bfloat16)
    parts = lax.psum_scatter(parts, "ctx", scatter_dimension=0, tiled=True)
    parts = lax.psum_scatter(parts, "shard", scatter_dimension=0, tiled=True)
    both = pair_join(parts)
    return jnp.concatenate([both[0], both[1]], axis=1).astype(jnp.float32)


def local(tokens, block_order, w_qkv, qkv_bias, w_out, norm_gains, w_gate, w_up, w_down, cotangent):
    groups, local_len, model_width = tokens.shape
    kv_width = KV_HEADS * HEAD_DIM
    repeats = Q_HEADS // KV_HEADS
    ctx_count = lax.axis_size("ctx")
    shard_count = lax.axis_size("shard")
    replica_count = lax.axis_size("replica")
    ctx_index = lax.axis_index("ctx")
    shard_index = lax.axis_index("shard")
    replica_index = lax.axis_index("replica")
    owner_index = ctx_index * shard_count + shard_index
    block_len = local_len // 2
    row_count = groups * local_len
    own_rows, ff_width = w_gate.shape
    own_ff = w_down.shape[0]
    half_ff = own_ff // replica_count
    slice_ff = shard_count * half_ff
    qkv_width = w_qkv.shape[1]
    f32, bf16 = jnp.float32, jnp.bfloat16
    everyone = ("ctx", "shard", "replica")

    slots = jnp.arange(SEQ_LEN, dtype=jnp.int32)
    owners = (
        (slots // block_len)[:, None] == jnp.arange(2 * ctx_count, dtype=jnp.int32)[None, :]
    ).astype(jnp.int32)
    positions = (
        jnp.sum(block_order[:, None, :] * owners[None], axis=-1) * block_len + slots % block_len
    )
    own_positions = lax.dynamic_slice_in_dim(positions, ctx_index * local_len, local_len, 1)

    extra = jnp.concatenate([qkv_bias, norm_gains.reshape(-1)])
    extra = jnp.pad(extra, (0, qkv_width - extra.shape[0]))
    packed = lax.all_gather(
        jnp.concatenate([w_qkv, extra[None]], axis=0), ("ctx", "shard"), axis=0, tiled=False
    )
    qkv_full = packed[:, :own_rows].reshape(model_width, qkv_width)
    extras = packed[:, own_rows]
    bias_len = qkv_bias.shape[0]
    bias_full = extras[:, :bias_len].reshape(-1)
    gains_full = (
        extras[:, bias_len : bias_len + 2 * own_rows]
        .reshape(-1, 2, own_rows)
        .transpose(1, 0, 2)
        .reshape(2, model_width)
    )
    out_full = lax.all_gather(w_out, ("ctx", "shard"), axis=0, tiled=True)

    def unit_slice(weight):
        own = lax.dynamic_index_in_dim(
            weight.reshape(own_rows, ctx_count, shard_count, replica_count, half_ff),
            replica_index,
            3,
            keepdims=False,
        )
        return own.reshape(own_rows, ctx_count, slice_ff).transpose(1, 0, 2)

    gate_up = jnp.stack([unit_slice(w_gate), unit_slice(w_up)], axis=1)
    gate_up = lax.all_to_all(gate_up, "ctx", split_axis=0, concat_axis=0, tiled=True)
    gate_up = lax.all_gather(gate_up, "shard", axis=0, tiled=False)
    gate_up = gate_up.transpose(2, 1, 0, 3, 4).reshape(2, model_width, slice_ff)
    gate_part, up_part = gate_up[0], gate_up[1]
    down_part = lax.all_gather(
        lax.dynamic_slice_in_dim(w_down, replica_index * half_ff, half_ff, 0),
        "shard",
        axis=0,
        tiled=True,
    )
    grad_top = cotangent.reshape(row_count, model_width)
    top_all = lax.all_gather(grad_top, ("ctx", "replica"), axis=0, tiled=True)

    gain_rows = gains_full.astype(f32)
    resid = tokens.reshape(row_count, model_width).astype(f32)
    first_inv = lax.rsqrt(jnp.mean(resid * resid, axis=-1, keepdims=True) + epsilon)
    normed_one = (resid * first_inv * gain_rows[0]).astype(bf16)
    projected = jnp.dot(normed_one, qkv_full, preferred_element_type=f32) + bias_full.astype(f32)
    cosine, sine = rope_tables(own_positions.reshape(row_count))
    query_rows = rotate(
        projected[:, :model_width].reshape(row_count, KV_HEADS, repeats, HEAD_DIM),
        cosine[:, None, None, :],
        sine[:, None, None, :],
    ).astype(bf16)
    key_rows = rotate(
        projected[:, model_width : model_width + kv_width].reshape(row_count, KV_HEADS, HEAD_DIM),
        cosine[:, None, :],
        sine[:, None, :],
    ).astype(bf16)
    value_rows = projected[:, model_width + kv_width :].astype(bf16)
    kv_local = jnp.concatenate([key_rows.reshape(row_count, kv_width), value_rows], axis=-1)
    kv_all = lax.all_gather(
        kv_local.reshape(groups, local_len, 2 * kv_width), "ctx", axis=1, tiled=True
    )
    all_keys = kv_all[..., :kv_width].reshape(groups, SEQ_LEN, KV_HEADS, HEAD_DIM)
    all_values = kv_all[..., kv_width:].reshape(groups, SEQ_LEN, KV_HEADS, HEAD_DIM)
    query_seq = query_rows.reshape(groups, local_len, KV_HEADS, repeats, HEAD_DIM)
    attended, logsum = lax.map(
        attend, (query_seq, all_keys, all_values, own_positions, positions)
    )
    attn_rows = attended.reshape(row_count, model_width).astype(bf16)
    middle = resid + jnp.dot(attn_rows, out_full, preferred_element_type=f32)
    second_inv = lax.rsqrt(jnp.mean(middle * middle, axis=-1, keepdims=True) + epsilon)
    normed_two = (middle * second_inv * gain_rows[1]).astype(bf16)

    normed_all = lax.all_gather(normed_two, ("ctx", "replica"), axis=0, tiled=True)
    gate_pre = jnp.dot(normed_all, gate_part, preferred_element_type=f32)
    up_pre = jnp.dot(normed_all, up_part, preferred_element_type=f32)
    grad_act = jnp.einsum("td,fd->tf", top_all, down_part, preferred_element_type=f32)
    sigmoid_gate = jax.nn.sigmoid(gate_pre)
    act_rows = (gate_pre * sigmoid_gate * up_pre).astype(bf16)
    grad_gate_rows = (
        grad_act * up_pre * sigmoid_gate * (1.0 + gate_pre * (1.0 - sigmoid_gate))
    ).astype(bf16)
    grad_up_rows = (grad_act * gate_pre * sigmoid_gate).astype(bf16)
    norm_part = jnp.einsum(
        "tf,df->td", grad_gate_rows, gate_part, preferred_element_type=f32
    ) + jnp.einsum("tf,df->td", grad_up_rows, up_part, preferred_element_type=f32)
    grad_norm_two = scatter_rows(norm_part).astype(f32)
    out_part = jnp.dot(act_rows, down_part, preferred_element_type=f32)
    block_out = (
        (middle + scatter_rows(out_part).astype(f32))
        .astype(bf16)
        .reshape(groups, local_len, model_width)
    )

    grad_gate = jnp.einsum("td,tf->df", normed_all, grad_gate_rows, preferred_element_type=f32)
    grad_up = jnp.einsum("td,tf->df", normed_all, grad_up_rows, preferred_element_type=f32)
    grad_down = jnp.einsum("tf,td->fd", act_rows, top_all, preferred_element_type=f32)
    down_sum = lax.psum_scatter(
        grad_down.astype(bf16), "shard", scatter_dimension=0, tiled=True
    )
    grad_down = pair_join(down_sum).reshape(own_ff, model_width).astype(f32)
    pair = jnp.stack(
        [
            grad_gate.astype(bf16).reshape(ctx_count, shard_count, own_rows, slice_ff),
            grad_up.astype(bf16).reshape(ctx_count, shard_count, own_rows, slice_ff),
        ]
    ).transpose(2, 1, 0, 3, 4)
    pair = lax.psum_scatter(pair, "shard", scatter_dimension=0, tiled=False)
    pair = lax.all_to_all(pair, "ctx", split_axis=0, concat_axis=0, tiled=True)
    pair = pair_join(pair)
    pair = (
        pair.reshape(replica_count, ctx_count, 2, own_rows, shard_count, half_ff)
        .transpose(2, 3, 1, 4, 0, 5)
        .reshape(2, own_rows, ff_width)
        .astype(f32)
    )

    gain_two, grad_middle = norm_back(middle, second_inv, gain_rows[1], grad_norm_two)
    grad_middle = grad_middle + grad_top.astype(f32)
    branch_rows = grad_middle.astype(bf16)
    grad_out = jnp.einsum("td,te->de", attn_rows, branch_rows, preferred_element_type=f32)
    grad_attended = jnp.einsum(
        "te,de->td", branch_rows, out_full, preferred_element_type=f32
    ).astype(bf16)
    grad_query, grad_key, grad_value = lax.map(
        attend_back,
        (
            query_seq,
            all_keys,
            all_values,
            grad_attended.reshape(groups, local_len, KV_HEADS, repeats, HEAD_DIM),
            logsum,
            own_positions,
            positions,
        ),
    )
    kv_grad = jnp.concatenate(
        [
            grad_key.reshape(groups, SEQ_LEN, kv_width),
            grad_value.reshape(groups, SEQ_LEN, kv_width),
        ],
        axis=-1,
    ).astype(bf16)
    own_kv = lax.psum_scatter(kv_grad, "ctx", scatter_dimension=1, tiled=True).astype(f32)
    own_kv = own_kv.reshape(row_count, 2 * kv_width)
    query_back = rotate_back(
        grad_query.reshape(row_count, KV_HEADS, repeats, HEAD_DIM),
        cosine[:, None, None, :],
        sine[:, None, None, :],
    ).reshape(row_count, model_width)
    key_back = rotate_back(
        own_kv[:, :kv_width].reshape(row_count, KV_HEADS, HEAD_DIM),
        cosine[:, None, :],
        sine[:, None, :],
    ).reshape(row_count, kv_width)
    grad_proj = jnp.concatenate([query_back, key_back, own_kv[:, kv_width:]], axis=-1).astype(bf16)
    grad_qkv = jnp.einsum("td,te->de", normed_one, grad_proj, preferred_element_type=f32)
    grad_bias = jnp.sum(grad_proj, axis=0, dtype=f32)
    grad_norm_one = jnp.einsum("te,de->td", grad_proj, qkv_full, preferred_element_type=f32)
    gain_one, grad_first = norm_back(resid, first_inv, gain_rows[0], grad_norm_one)
    input_grad = (grad_middle + grad_first).reshape(groups, local_len, model_width)
    small = lax.psum(jnp.concatenate([grad_bias, gain_one, gain_two]), everyone)
    bias_sum = lax.dynamic_slice_in_dim(small[:qkv_width], owner_index * bias_len, bias_len, 0)
    gain_sum = lax.dynamic_slice_in_dim(
        small[qkv_width:].reshape(2, model_width), owner_index * own_rows, own_rows, 1
    )
    return (
        block_out,
        input_grad,
        owner_sum(grad_qkv),
        bias_sum,
        owner_sum(grad_out),
        gain_sum,
        pair[0],
        pair[1],
        grad_down,
    )


def solution(mesh):
    placed = (
        P(("shard", "replica"), "ctx", None),
        P(("shard", "replica"), None),
        P(("ctx", "shard"), None),
        P(("ctx", "shard")),
        P(("ctx", "shard"), None),
        P(None, ("ctx", "shard")),
        P(("ctx", "shard"), None),
        P(("ctx", "shard"), None),
        P(("ctx", "shard"), None),
        P(("shard", "replica"), "ctx", None),
    )
    return jax.shard_map(
        local,
        mesh=mesh,
        in_specs=placed,
        out_specs=(
            P(("shard", "replica"), "ctx", None),
            P(("shard", "replica"), "ctx", None),
            P(("ctx", "shard"), None),
            P(("ctx", "shard")),
            P(("ctx", "shard"), None),
            P(None, ("ctx", "shard")),
            P(("ctx", "shard"), None),
            P(("ctx", "shard"), None),
            P(("ctx", "shard"), None),
        ),
        check_vma=False,
    )
```

```python
import jax
import jax.numpy as jnp
from jax import lax
from jax.sharding import PartitionSpec as P

Q_HEADS = 14
KV_HEADS = 2
HEAD_DIM = 64
SEQ_LEN = 1024


epsilon = 1e-06
rope_base = 1000000.0
score_scale = 0.125
masked_value = -1e30


def rope_tables(positions):
    half_dim = HEAD_DIM // 2
    inverse = rope_base ** (-(jnp.arange(half_dim, dtype=jnp.float32) * 2.0) / HEAD_DIM)
    angles = positions.astype(jnp.float32)[..., None] * inverse
    angles = jnp.concatenate([angles, angles], axis=-1)
    return (jnp.cos(angles), jnp.sin(angles))


def rotate(values, cosine, sine):
    half_dim = values.shape[-1] // 2
    turned = jnp.concatenate([-values[..., half_dim:], values[..., :half_dim]], axis=-1)
    return values * cosine + turned * sine


def rotate_back(grads, cosine, sine):
    half_dim = grads.shape[-1] // 2
    moved = grads * sine
    turned = jnp.concatenate([moved[..., half_dim:], -moved[..., :half_dim]], axis=-1)
    return grads * cosine + turned


def norm_back(inputs, inverse, gain, upstream):
    scaled = upstream * gain
    gain_term = jnp.sum(upstream * inputs * inverse, axis=0)
    input_term = inverse * scaled - inputs * inverse**3 * jnp.mean(
        scaled * inputs, axis=-1, keepdims=True
    )
    return (gain_term, input_term)


def masked_scores(queries, key_rows, pos_query, pos_key):
    scores = (
        jnp.einsum("qhrd,khd->hrqk", queries, key_rows, preferred_element_type=jnp.float32)
        * score_scale
    )
    allowed = pos_query[:, None] >= pos_key[None, :]
    return jnp.where(allowed, scores, masked_value)


def attend(packed):
    queries, key_rows, value_rows, pos_query, pos_key = packed
    scores = masked_scores(queries, key_rows, pos_query, pos_key)
    top_score = jnp.max(scores, axis=-1, keepdims=True)
    weights = jnp.exp(scores - top_score)
    totals = jnp.sum(weights, axis=-1, keepdims=True)
    attn_probs = (weights / totals).astype(jnp.bfloat16)
    mixed_out = jnp.einsum(
        "hrqk,khd->qhrd", attn_probs, value_rows, preferred_element_type=jnp.float32
    )
    return (mixed_out, top_score + jnp.log(totals))


def attend_back(packed):
    queries, key_rows, value_rows, upstream, logsum, pos_query, pos_key = packed
    scores = masked_scores(queries, key_rows, pos_query, pos_key)
    attn_probs = jnp.exp(scores - logsum)
    dprob = jnp.einsum("qhrd,khd->hrqk", upstream, value_rows, preferred_element_type=jnp.float32)
    row_dot = jnp.sum(attn_probs * dprob, axis=-1, keepdims=True)
    dscore = (attn_probs * (dprob - row_dot)).astype(jnp.bfloat16)
    grad_query = (
        jnp.einsum("hrqk,khd->qhrd", dscore, key_rows, preferred_element_type=jnp.float32)
        * score_scale
    )
    grad_key = (
        jnp.einsum("hrqk,qhrd->khd", dscore, queries, preferred_element_type=jnp.float32)
        * score_scale
    )
    grad_value = jnp.einsum(
        "hrqk,qhrd->khd",
        attn_probs.astype(jnp.bfloat16),
        upstream,
        preferred_element_type=jnp.float32,
    )
    return (grad_query, grad_key, grad_value)


def reverse_bits(value, count):
    return sum(((value >> at) & 1) << (count - 1 - at) for at in range(count))


def ctx_steps():
    count = lax.axis_size("ctx").bit_length() - 1
    replica = lax.axis_index("replica")
    index = lax.axis_index("ctx")
    index = jnp.where(replica == 0, index, reverse_bits(index, count))
    steps = []
    for at in reversed(range(count)):
        masks = (1 << at, 1 << (count - 1 - at))
        pairs = [
            (ctx * 2 + core, (ctx ^ masks[core]) * 2 + core)
            for ctx in range(1 << count)
            for core in range(2)
        ]
        steps.append((("ctx", "replica"), pairs, (index >> at) & 1))
    return steps


def axis_steps(name):
    size = lax.axis_size(name)
    index = lax.axis_index(name)
    return [
        (name, [(own, own ^ (1 << at)) for own in range(size)], (index >> at) & 1)
        for at in reversed(range(size.bit_length() - 1))
    ]


def core_order(parts):
    count = parts.shape[0].bit_length() - 1
    rest = parts.shape[1:]
    dims = tuple(reversed(range(count))) + tuple(range(count, count + len(rest)))
    turned = parts.reshape((2,) * count + rest).transpose(dims).reshape(parts.shape)
    return jnp.where(lax.axis_index("replica") == 0, parts, turned)


def halve(parts, step):
    names, pairs, bit = step
    split = parts.reshape((2, parts.shape[0] // 2) + parts.shape[1:])
    kept = lax.dynamic_index_in_dim(split, bit, 0, keepdims=False)
    sent = lax.dynamic_index_in_dim(split, 1 - bit, 0, keepdims=False)
    arrived = lax.ppermute(sent.astype(jnp.bfloat16), names, pairs)
    return kept.astype(jnp.float32) + arrived.astype(jnp.float32)


def double(parts, step):
    names, pairs, bit = step
    other = lax.ppermute(parts, names, pairs)
    return jnp.concatenate([jnp.where(bit == 0, parts, other), jnp.where(bit == 0, other, parts)])


def pair_join(values):
    return double(values[None], axis_steps("replica")[0])


def gather_group(rows):
    for names, pairs, _ in ctx_steps() + axis_steps("replica"):
        rows = jnp.concatenate([rows, lax.ppermute(rows, names, pairs)])
    return rows


def scatter_group(rows):
    for names, pairs, _ in reversed(ctx_steps() + axis_steps("replica")):
        half = rows.shape[0] // 2
        arrived = lax.ppermute(rows[half:].astype(jnp.bfloat16), names, pairs)
        rows = rows[:half] + arrived.astype(jnp.float32)
    return rows


def gather_owners(own):
    rows, width = own.shape
    halves = own.reshape(rows, 2, width // 2)
    parts = lax.dynamic_index_in_dim(halves, lax.axis_index("replica"), 1, keepdims=False)[None]
    for step in reversed(axis_steps("shard")):
        parts = double(parts, step)
    parts = parts[None]
    for step in reversed(ctx_steps()):
        parts = double(parts, step)
    parts = core_order(parts)
    both = pair_join(parts.reshape(-1, width // 2))
    return jnp.concatenate([both[0], both[1]], axis=1)


def owner_sum(grad):
    rows, width = grad.shape
    ctx_count = lax.axis_size("ctx")
    shard_count = lax.axis_size("shard")
    halves = grad.reshape(rows, 2, width // 2).transpose(1, 0, 2)
    parts = halve(halves, axis_steps("replica")[0])
    parts = core_order(parts.reshape(ctx_count, shard_count, -1, width // 2))
    for step in ctx_steps():
        parts = halve(parts, step)
    parts = parts[0]
    for step in axis_steps("shard"):
        parts = halve(parts, step)
    both = pair_join(parts[0].astype(jnp.bfloat16))
    return jnp.concatenate([both[0], both[1]], axis=1).astype(jnp.float32)


def local(tokens, block_order, w_qkv, qkv_bias, w_out, norm_gains, w_gate, w_up, w_down, cotangent):
    groups, local_len, model_width = tokens.shape
    kv_width = KV_HEADS * HEAD_DIM
    repeats = Q_HEADS // KV_HEADS
    ctx_count = lax.axis_size("ctx")
    shard_count = lax.axis_size("shard")
    replica_count = lax.axis_size("replica")
    ctx_index = lax.axis_index("ctx")
    replica_index = lax.axis_index("replica")
    block_len = local_len // 2
    row_count = groups * local_len
    own_rows, ff_width = w_gate.shape
    own_ff = w_down.shape[0]
    half_ff = own_ff // replica_count
    slice_ff = shard_count * half_ff
    qkv_width = w_qkv.shape[1]
    f32, bf16 = jnp.float32, jnp.bfloat16

    slots = jnp.arange(SEQ_LEN, dtype=jnp.int32)
    owners = (
        (slots // block_len)[:, None] == jnp.arange(2 * ctx_count, dtype=jnp.int32)[None, :]
    ).astype(jnp.int32)
    positions = (
        jnp.sum(block_order[:, None, :] * owners[None], axis=-1) * block_len + slots % block_len
    )
    own_positions = lax.dynamic_slice_in_dim(positions, ctx_index * local_len, local_len, 1)

    qkv_full = gather_owners(w_qkv)
    bias_len = qkv_bias.shape[0]
    extras = jnp.concatenate([qkv_bias, norm_gains.reshape(-1)])[None]
    for step in reversed(axis_steps("shard")):
        extras = double(extras, step)
    extras = extras[None]
    for step in reversed(ctx_steps()):
        extras = double(extras, step)
    extras = core_order(extras).reshape(ctx_count * shard_count, -1)
    bias_full = extras[:, :bias_len].reshape(-1)
    gains_full = (
        extras[:, bias_len:].reshape(-1, 2, own_rows).transpose(1, 0, 2).reshape(2, model_width)
    )
    out_full = gather_owners(w_out)

    def unit_slice(weight):
        own = lax.dynamic_index_in_dim(
            weight.reshape(own_rows, ctx_count, shard_count, replica_count, half_ff),
            replica_index,
            3,
            keepdims=False,
        )
        return own.reshape(own_rows, ctx_count, slice_ff).transpose(1, 0, 2)

    gate_up = jnp.stack([unit_slice(w_gate), unit_slice(w_up)], axis=1)
    gate_up = lax.all_to_all(gate_up, "ctx", split_axis=0, concat_axis=0, tiled=True)
    gate_up = lax.all_gather(gate_up, "shard", axis=0, tiled=False)
    gate_up = gate_up.transpose(2, 1, 0, 3, 4).reshape(2, model_width, slice_ff)
    gate_part, up_part = gate_up[0], gate_up[1]
    down_part = lax.all_gather(
        lax.dynamic_slice_in_dim(w_down, replica_index * half_ff, half_ff, 0),
        "shard",
        axis=0,
        tiled=True,
    )
    grad_top = cotangent.reshape(row_count, model_width)
    top_all = gather_group(grad_top)

    gain_rows = gains_full.astype(f32)
    resid = tokens.reshape(row_count, model_width).astype(f32)
    first_inv = lax.rsqrt(jnp.mean(resid * resid, axis=-1, keepdims=True) + epsilon)
    normed_one = (resid * first_inv * gain_rows[0]).astype(bf16)
    projected = jnp.dot(normed_one, qkv_full, preferred_element_type=f32) + bias_full.astype(f32)
    cosine, sine = rope_tables(own_positions.reshape(row_count))
    query_rows = rotate(
        projected[:, :model_width].reshape(row_count, KV_HEADS, repeats, HEAD_DIM),
        cosine[:, None, None, :],
        sine[:, None, None, :],
    ).astype(bf16)
    key_rows = rotate(
        projected[:, model_width : model_width + kv_width].reshape(row_count, KV_HEADS, HEAD_DIM),
        cosine[:, None, :],
        sine[:, None, :],
    ).astype(bf16)
    value_rows = projected[:, model_width + kv_width :].astype(bf16)
    kv_local = jnp.concatenate([key_rows.reshape(row_count, kv_width), value_rows], axis=-1)
    kv_all = lax.all_gather(
        kv_local.reshape(groups, local_len, 2 * kv_width), "ctx", axis=1, tiled=True
    )
    all_keys = kv_all[..., :kv_width].reshape(groups, SEQ_LEN, KV_HEADS, HEAD_DIM)
    all_values = kv_all[..., kv_width:].reshape(groups, SEQ_LEN, KV_HEADS, HEAD_DIM)
    query_seq = query_rows.reshape(groups, local_len, KV_HEADS, repeats, HEAD_DIM)
    attended, logsum = lax.map(
        attend, (query_seq, all_keys, all_values, own_positions, positions)
    )
    attn_rows = attended.reshape(row_count, model_width).astype(bf16)
    middle = resid + jnp.dot(attn_rows, out_full, preferred_element_type=f32)
    second_inv = lax.rsqrt(jnp.mean(middle * middle, axis=-1, keepdims=True) + epsilon)
    normed_two = (middle * second_inv * gain_rows[1]).astype(bf16)

    normed_all = gather_group(normed_two)
    gate_pre = jnp.dot(normed_all, gate_part, preferred_element_type=f32)
    up_pre = jnp.dot(normed_all, up_part, preferred_element_type=f32)
    grad_act = jnp.einsum("td,fd->tf", top_all, down_part, preferred_element_type=f32)
    sigmoid_gate = jax.nn.sigmoid(gate_pre)
    act_rows = (gate_pre * sigmoid_gate * up_pre).astype(bf16)
    grad_gate_rows = (
        grad_act * up_pre * sigmoid_gate * (1.0 + gate_pre * (1.0 - sigmoid_gate))
    ).astype(bf16)
    grad_up_rows = (grad_act * gate_pre * sigmoid_gate).astype(bf16)
    norm_part = jnp.einsum(
        "tf,df->td", grad_gate_rows, gate_part, preferred_element_type=f32
    ) + jnp.einsum("tf,df->td", grad_up_rows, up_part, preferred_element_type=f32)
    grad_norm_two = scatter_group(norm_part)
    out_part = jnp.dot(act_rows, down_part, preferred_element_type=f32)
    block_out = (
        (middle + scatter_group(out_part))
        .astype(bf16)
        .reshape(groups, local_len, model_width)
    )

    grad_gate = jnp.einsum("td,tf->df", normed_all, grad_gate_rows, preferred_element_type=f32)
    grad_up = jnp.einsum("td,tf->df", normed_all, grad_up_rows, preferred_element_type=f32)
    grad_down = jnp.einsum("tf,td->fd", act_rows, top_all, preferred_element_type=f32)
    pair = jnp.stack(
        [
            grad_gate.astype(bf16).reshape(ctx_count, shard_count, own_rows, slice_ff),
            grad_up.astype(bf16).reshape(ctx_count, shard_count, own_rows, slice_ff),
        ]
    ).transpose(2, 1, 0, 3, 4)
    pair = lax.psum_scatter(
        pair.reshape(-1, slice_ff), "shard", scatter_dimension=0, tiled=True
    ).reshape(ctx_count, 2, own_rows, slice_ff)
    pair, grad_down = lax.optimization_barrier((pair, grad_down.astype(bf16)))
    down_sum = lax.psum_scatter(grad_down, "shard", scatter_dimension=0, tiled=True)
    grad_down = pair_join(down_sum).reshape(own_ff, model_width).astype(f32)
    pair = lax.all_to_all(pair, "ctx", split_axis=0, concat_axis=0, tiled=True)
    pair = pair_join(pair)
    pair = (
        pair.reshape(replica_count, ctx_count, 2, own_rows, shard_count, half_ff)
        .transpose(2, 3, 1, 4, 0, 5)
        .reshape(2, own_rows, ff_width)
        .astype(f32)
    )

    gain_two, grad_middle = norm_back(middle, second_inv, gain_rows[1], grad_norm_two)
    grad_middle = grad_middle + grad_top.astype(f32)
    branch_rows = grad_middle.astype(bf16)
    grad_out = jnp.einsum("td,te->de", attn_rows, branch_rows, preferred_element_type=f32)
    grad_attended = jnp.einsum(
        "te,de->td", branch_rows, out_full, preferred_element_type=f32
    ).astype(bf16)
    grad_query, grad_key, grad_value = lax.map(
        attend_back,
        (
            query_seq,
            all_keys,
            all_values,
            grad_attended.reshape(groups, local_len, KV_HEADS, repeats, HEAD_DIM),
            logsum,
            own_positions,
            positions,
        ),
    )
    kv_grad = jnp.concatenate(
        [
            grad_key.reshape(groups, SEQ_LEN, kv_width),
            grad_value.reshape(groups, SEQ_LEN, kv_width),
        ],
        axis=-1,
    )
    own_kv = core_order(
        kv_grad.reshape(groups, ctx_count, local_len, 2 * kv_width).transpose(1, 0, 2, 3)
    )
    for step in ctx_steps():
        own_kv = halve(own_kv, step)
    own_kv = own_kv.reshape(row_count, 2 * kv_width)
    query_back = rotate_back(
        grad_query.reshape(row_count, KV_HEADS, repeats, HEAD_DIM),
        cosine[:, None, None, :],
        sine[:, None, None, :],
    ).reshape(row_count, model_width)
    key_back = rotate_back(
        own_kv[:, :kv_width].reshape(row_count, KV_HEADS, HEAD_DIM),
        cosine[:, None, :],
        sine[:, None, :],
    ).reshape(row_count, kv_width)
    grad_proj = jnp.concatenate([query_back, key_back, own_kv[:, kv_width:]], axis=-1).astype(bf16)
    grad_qkv = jnp.einsum("td,te->de", normed_one, grad_proj, preferred_element_type=f32)
    grad_bias = jnp.sum(grad_proj, axis=0, dtype=f32)
    grad_norm_one = jnp.einsum("te,de->td", grad_proj, qkv_full, preferred_element_type=f32)
    gain_one, grad_first = norm_back(resid, first_inv, gain_rows[0], grad_norm_one)
    input_grad = (grad_middle + grad_first).reshape(groups, local_len, model_width)
    own_gains = jnp.stack([gain_one, gain_two]).reshape(2, -1, own_rows).transpose(1, 0, 2)
    small = jnp.concatenate(
        [grad_bias.reshape(-1, bias_len), own_gains.reshape(-1, 2 * own_rows)], axis=1
    )
    name, pairs, _ = axis_steps("replica")[0]
    small = small + lax.ppermute(small, name, pairs)
    small = core_order(small.reshape(ctx_count, shard_count, -1))
    for step in ctx_steps():
        small = halve(small, step)
    small = small[0]
    for step in axis_steps("shard"):
        small = halve(small, step)
    bias_sum = small[0, :bias_len]
    gain_sum = small[0, bias_len:].reshape(2, own_rows)
    return (
        block_out,
        input_grad,
        owner_sum(grad_qkv),
        bias_sum,
        owner_sum(grad_out),
        gain_sum,
        pair[0],
        pair[1],
        grad_down,
    )


def solution(mesh):
    placed = (
        P(("shard", "replica"), "ctx", None),
        P(("shard", "replica"), None),
        P(("ctx", "shard"), None),
        P(("ctx", "shard")),
        P(("ctx", "shard"), None),
        P(None, ("ctx", "shard")),
        P(("ctx", "shard"), None),
        P(("ctx", "shard"), None),
        P(("ctx", "shard"), None),
        P(("shard", "replica"), "ctx", None),
    )
    return jax.shard_map(
        local,
        mesh=mesh,
        in_specs=placed,
        out_specs=(
            P(("shard", "replica"), "ctx", None),
            P(("shard", "replica"), "ctx", None),
            P(("ctx", "shard"), None),
            P(("ctx", "shard")),
            P(("ctx", "shard"), None),
            P(None, ("ctx", "shard")),
            P(("ctx", "shard"), None),
            P(("ctx", "shard"), None),
            P(("ctx", "shard"), None),
        ),
        check_vma=False,
    )
```

```python
import jax
import jax.numpy as jnp
from jax import lax
from jax.sharding import PartitionSpec as P

Q_HEADS = 14
KV_HEADS = 2
HEAD_DIM = 64
SEQ_LEN = 1024


epsilon = 1e-06
rope_base = 1000000.0
score_scale = 0.125
masked_value = -1e30


def rope_tables(positions):
    half_dim = HEAD_DIM // 2
    inverse = rope_base ** (-(jnp.arange(half_dim, dtype=jnp.float32) * 2.0) / HEAD_DIM)
    angles = positions.astype(jnp.float32)[..., None] * inverse
    angles = jnp.concatenate([angles, angles], axis=-1)
    return (jnp.cos(angles), jnp.sin(angles))


def rotate(values, cosine, sine):
    half_dim = values.shape[-1] // 2
    turned = jnp.concatenate([-values[..., half_dim:], values[..., :half_dim]], axis=-1)
    return values * cosine + turned * sine


def rotate_back(grads, cosine, sine):
    half_dim = grads.shape[-1] // 2
    moved = grads * sine
    turned = jnp.concatenate([moved[..., half_dim:], -moved[..., :half_dim]], axis=-1)
    return grads * cosine + turned


def norm_back(inputs, inverse, gain, upstream):
    scaled = upstream * gain
    gain_term = jnp.sum(upstream * inputs * inverse, axis=0)
    input_term = inverse * scaled - inputs * inverse**3 * jnp.mean(
        scaled * inputs, axis=-1, keepdims=True
    )
    return (gain_term, input_term)


def masked_scores(queries, key_rows, pos_query, pos_key):
    scores = (
        jnp.einsum("qhrd,khd->hrqk", queries, key_rows, preferred_element_type=jnp.float32)
        * score_scale
    )
    allowed = pos_query[:, None] >= pos_key[None, :]
    return jnp.where(allowed, scores, masked_value)


def attend(packed):
    queries, key_rows, value_rows, pos_query, pos_key = packed
    scores = masked_scores(queries, key_rows, pos_query, pos_key)
    top_score = jnp.max(scores, axis=-1, keepdims=True)
    weights = jnp.exp(scores - top_score)
    totals = jnp.sum(weights, axis=-1, keepdims=True)
    attn_probs = (weights / totals).astype(jnp.bfloat16)
    mixed_out = jnp.einsum(
        "hrqk,khd->qhrd", attn_probs, value_rows, preferred_element_type=jnp.float32
    )
    return (mixed_out, top_score + jnp.log(totals))


def attend_back(packed):
    queries, key_rows, value_rows, upstream, logsum, pos_query, pos_key = packed
    scores = masked_scores(queries, key_rows, pos_query, pos_key)
    attn_probs = jnp.exp(scores - logsum)
    dprob = jnp.einsum("qhrd,khd->hrqk", upstream, value_rows, preferred_element_type=jnp.float32)
    row_dot = jnp.sum(attn_probs * dprob, axis=-1, keepdims=True)
    dscore = (attn_probs * (dprob - row_dot)).astype(jnp.bfloat16)
    grad_query = (
        jnp.einsum("hrqk,khd->qhrd", dscore, key_rows, preferred_element_type=jnp.float32)
        * score_scale
    )
    grad_key = (
        jnp.einsum("hrqk,qhrd->khd", dscore, queries, preferred_element_type=jnp.float32)
        * score_scale
    )
    grad_value = jnp.einsum(
        "hrqk,qhrd->khd",
        attn_probs.astype(jnp.bfloat16),
        upstream,
        preferred_element_type=jnp.float32,
    )
    return (grad_query, grad_key, grad_value)


def reverse_bits(value, count):
    return sum(((value >> at) & 1) << (count - 1 - at) for at in range(count))


def ctx_steps():
    count = lax.axis_size("ctx").bit_length() - 1
    replica = lax.axis_index("replica")
    index = lax.axis_index("ctx")
    index = jnp.where(replica == 0, index, reverse_bits(index, count))
    steps = []
    for at in reversed(range(count)):
        masks = (1 << at, 1 << (count - 1 - at))
        pairs = [
            (ctx * 2 + core, (ctx ^ masks[core]) * 2 + core)
            for ctx in range(1 << count)
            for core in range(2)
        ]
        steps.append((("ctx", "replica"), pairs, (index >> at) & 1))
    return steps


def axis_steps(name):
    size = lax.axis_size(name)
    index = lax.axis_index(name)
    return [
        (name, [(own, own ^ (1 << at)) for own in range(size)], (index >> at) & 1)
        for at in reversed(range(size.bit_length() - 1))
    ]


def core_order(parts):
    count = parts.shape[0].bit_length() - 1
    rest = parts.shape[1:]
    dims = tuple(reversed(range(count))) + tuple(range(count, count + len(rest)))
    turned = parts.reshape((2,) * count + rest).transpose(dims).reshape(parts.shape)
    return jnp.where(lax.axis_index("replica") == 0, parts, turned)


def halve(parts, step):
    names, pairs, bit = step
    split = parts.reshape((2, parts.shape[0] // 2) + parts.shape[1:])
    kept = lax.dynamic_index_in_dim(split, bit, 0, keepdims=False)
    sent = lax.dynamic_index_in_dim(split, 1 - bit, 0, keepdims=False)
    arrived = lax.ppermute(sent.astype(jnp.bfloat16), names, pairs)
    return kept.astype(jnp.float32) + arrived.astype(jnp.float32)


def double(parts, step):
    names, pairs, bit = step
    other = lax.ppermute(parts, names, pairs)
    return jnp.concatenate([jnp.where(bit == 0, parts, other), jnp.where(bit == 0, other, parts)])


def gather_shards(own):
    steps = axis_steps("shard")
    parts = own.reshape((1,) * len(steps) + own.shape)
    for at, (name, pairs, bit) in enumerate(steps):
        other = lax.ppermute(parts, name, pairs)
        parts = jnp.concatenate(
            [jnp.where(bit == 0, parts, other), jnp.where(bit == 0, other, parts)], axis=at
        )
    return parts.reshape((-1,) + own.shape[1:])


def scatter_shards(rows):
    steps = axis_steps("shard")
    parts = rows.reshape((2,) * len(steps) + (-1,) + rows.shape[1:])
    for at, (name, pairs, bit) in reversed(list(enumerate(steps))):
        kept = lax.dynamic_index_in_dim(parts, bit, at, keepdims=False)
        sent = lax.dynamic_index_in_dim(parts, 1 - bit, at, keepdims=False)
        arrived = lax.ppermute(sent.astype(jnp.bfloat16), name, pairs)
        parts = kept.astype(jnp.float32) + arrived.astype(jnp.float32)
    return parts


def pair_join(values):
    return double(values[None], axis_steps("replica")[0])


def gather_group(rows):
    for names, pairs, _ in ctx_steps() + axis_steps("replica"):
        rows = jnp.concatenate([rows, lax.ppermute(rows, names, pairs)])
    return rows


def scatter_group(rows):
    for names, pairs, _ in reversed(ctx_steps() + axis_steps("replica")):
        half = rows.shape[0] // 2
        arrived = lax.ppermute(rows[half:].astype(jnp.bfloat16), names, pairs)
        rows = rows[:half] + arrived.astype(jnp.float32)
    return rows


def gather_owners(own):
    rows, width = own.shape
    halves = own.reshape(rows, 2, width // 2)
    parts = lax.dynamic_index_in_dim(halves, lax.axis_index("replica"), 1, keepdims=False)[None]
    for step in reversed(axis_steps("shard")):
        parts = double(parts, step)
    parts = parts[None]
    for step in reversed(ctx_steps()):
        parts = double(parts, step)
    parts = core_order(parts)
    both = pair_join(parts.reshape(-1, width // 2))
    return jnp.concatenate([both[0], both[1]], axis=1)


def owner_sum(grad):
    rows, width = grad.shape
    ctx_count = lax.axis_size("ctx")
    shard_count = lax.axis_size("shard")
    halves = grad.reshape(rows, 2, width // 2).transpose(1, 0, 2)
    parts = halve(halves, axis_steps("replica")[0])
    parts = core_order(parts.reshape(ctx_count, shard_count, -1, width // 2))
    for step in ctx_steps():
        parts = halve(parts, step)
    parts = parts[0]
    for step in axis_steps("shard"):
        parts = halve(parts, step)
    both = pair_join(parts[0].astype(jnp.bfloat16))
    return jnp.concatenate([both[0], both[1]], axis=1).astype(jnp.float32)


def local(tokens, block_order, w_qkv, qkv_bias, w_out, norm_gains, w_gate, w_up, w_down, cotangent):
    groups, local_len, model_width = tokens.shape
    kv_width = KV_HEADS * HEAD_DIM
    repeats = Q_HEADS // KV_HEADS
    ctx_count = lax.axis_size("ctx")
    shard_count = lax.axis_size("shard")
    replica_count = lax.axis_size("replica")
    ctx_index = lax.axis_index("ctx")
    replica_index = lax.axis_index("replica")
    block_len = local_len // 2
    row_count = groups * local_len
    own_rows, ff_width = w_gate.shape
    own_ff = w_down.shape[0]
    half_ff = own_ff // replica_count
    slice_ff = shard_count * half_ff
    qkv_width = w_qkv.shape[1]
    f32, bf16 = jnp.float32, jnp.bfloat16

    slots = jnp.arange(SEQ_LEN, dtype=jnp.int32)
    owners = (
        (slots // block_len)[:, None] == jnp.arange(2 * ctx_count, dtype=jnp.int32)[None, :]
    ).astype(jnp.int32)
    positions = (
        jnp.sum(block_order[:, None, :] * owners[None], axis=-1) * block_len + slots % block_len
    )
    own_positions = lax.dynamic_slice_in_dim(positions, ctx_index * local_len, local_len, 1)

    qkv_full = gather_owners(w_qkv)
    bias_len = qkv_bias.shape[0]
    extras = jnp.concatenate([qkv_bias, norm_gains.reshape(-1)])[None]
    for step in reversed(axis_steps("shard")):
        extras = double(extras, step)
    extras = extras[None]
    for step in reversed(ctx_steps()):
        extras = double(extras, step)
    extras = core_order(extras).reshape(ctx_count * shard_count, -1)
    bias_full = extras[:, :bias_len].reshape(-1)
    gains_full = (
        extras[:, bias_len:].reshape(-1, 2, own_rows).transpose(1, 0, 2).reshape(2, model_width)
    )
    qkv_full, w_out, w_down, cotangent = lax.optimization_barrier(
        (qkv_full, w_out, w_down, cotangent)
    )
    out_full = gather_owners(w_out)

    def unit_slice(weight):
        own = lax.dynamic_index_in_dim(
            weight.reshape(own_rows, ctx_count, shard_count, replica_count, half_ff),
            replica_index,
            3,
            keepdims=False,
        )
        return own.reshape(own_rows, ctx_count, slice_ff).transpose(1, 0, 2)

    gate_up = jnp.stack([unit_slice(w_gate), unit_slice(w_up)], axis=1)
    gate_up = lax.all_to_all(gate_up, "ctx", split_axis=0, concat_axis=0, tiled=True)
    gate_up = lax.all_gather(gate_up, "shard", axis=0, tiled=False)
    gate_up = gate_up.transpose(2, 1, 0, 3, 4).reshape(2, model_width, slice_ff)
    gate_part, up_part = gate_up[0], gate_up[1]
    down_part = gather_shards(
        lax.dynamic_slice_in_dim(w_down, replica_index * half_ff, half_ff, 0)
    )
    grad_top = cotangent.reshape(row_count, model_width)
    top_all = gather_group(grad_top)

    gain_rows = gains_full.astype(f32)
    resid = tokens.reshape(row_count, model_width).astype(f32)
    first_inv = lax.rsqrt(jnp.mean(resid * resid, axis=-1, keepdims=True) + epsilon)
    normed_one = (resid * first_inv * gain_rows[0]).astype(bf16)
    projected = jnp.dot(normed_one, qkv_full, preferred_element_type=f32) + bias_full.astype(f32)
    cosine, sine = rope_tables(own_positions.reshape(row_count))
    query_rows = rotate(
        projected[:, :model_width].reshape(row_count, KV_HEADS, repeats, HEAD_DIM),
        cosine[:, None, None, :],
        sine[:, None, None, :],
    ).astype(bf16)
    key_rows = rotate(
        projected[:, model_width : model_width + kv_width].reshape(row_count, KV_HEADS, HEAD_DIM),
        cosine[:, None, :],
        sine[:, None, :],
    ).astype(bf16)
    value_rows = projected[:, model_width + kv_width :].astype(bf16)
    kv_local = jnp.concatenate([key_rows.reshape(row_count, kv_width), value_rows], axis=-1)
    kv_all = lax.all_gather(
        kv_local.reshape(groups, local_len, 2 * kv_width), "ctx", axis=1, tiled=True
    )
    all_keys = kv_all[..., :kv_width].reshape(groups, SEQ_LEN, KV_HEADS, HEAD_DIM)
    all_values = kv_all[..., kv_width:].reshape(groups, SEQ_LEN, KV_HEADS, HEAD_DIM)
    query_seq = query_rows.reshape(groups, local_len, KV_HEADS, repeats, HEAD_DIM)
    attended, logsum = lax.map(
        attend, (query_seq, all_keys, all_values, own_positions, positions)
    )
    attn_rows = attended.reshape(row_count, model_width).astype(bf16)
    middle = resid + jnp.dot(attn_rows, out_full, preferred_element_type=f32)
    second_inv = lax.rsqrt(jnp.mean(middle * middle, axis=-1, keepdims=True) + epsilon)
    normed_two = (middle * second_inv * gain_rows[1]).astype(bf16)

    normed_all = gather_group(normed_two)
    gate_pre = jnp.dot(normed_all, gate_part, preferred_element_type=f32)
    up_pre = jnp.dot(normed_all, up_part, preferred_element_type=f32)
    grad_act = jnp.einsum("td,fd->tf", top_all, down_part, preferred_element_type=f32)
    sigmoid_gate = jax.nn.sigmoid(gate_pre)
    act_rows = (gate_pre * sigmoid_gate * up_pre).astype(bf16)
    grad_gate_rows = (
        grad_act * up_pre * sigmoid_gate * (1.0 + gate_pre * (1.0 - sigmoid_gate))
    ).astype(bf16)
    grad_up_rows = (grad_act * gate_pre * sigmoid_gate).astype(bf16)
    norm_part = jnp.einsum(
        "tf,df->td", grad_gate_rows, gate_part, preferred_element_type=f32
    ) + jnp.einsum("tf,df->td", grad_up_rows, up_part, preferred_element_type=f32)
    grad_norm_two = scatter_group(norm_part)
    out_part = jnp.dot(act_rows, down_part, preferred_element_type=f32)
    out_part, grad_norm_two = lax.optimization_barrier((out_part, grad_norm_two))
    block_out = (
        (middle + scatter_group(out_part))
        .astype(bf16)
        .reshape(groups, local_len, model_width)
    )

    grad_gate = jnp.einsum("td,tf->df", normed_all, grad_gate_rows, preferred_element_type=f32)
    grad_up = jnp.einsum("td,tf->df", normed_all, grad_up_rows, preferred_element_type=f32)
    grad_down = jnp.einsum("tf,td->fd", act_rows, top_all, preferred_element_type=f32)
    pair = jnp.stack(
        [
            grad_gate.astype(bf16).reshape(ctx_count, shard_count, own_rows, slice_ff),
            grad_up.astype(bf16).reshape(ctx_count, shard_count, own_rows, slice_ff),
        ]
    ).transpose(2, 1, 0, 3, 4)
    pair = lax.psum_scatter(
        pair.reshape(-1, slice_ff), "shard", scatter_dimension=0, tiled=True
    ).reshape(ctx_count, 2, own_rows, slice_ff)
    down_sum = scatter_shards(grad_down)
    grad_down = pair_join(down_sum.astype(bf16)).reshape(own_ff, model_width).astype(f32)
    gain_two, grad_middle = norm_back(middle, second_inv, gain_rows[1], grad_norm_two)
    grad_middle = grad_middle + grad_top.astype(f32)
    branch_rows = grad_middle.astype(bf16)
    grad_out = jnp.einsum("td,te->de", attn_rows, branch_rows, preferred_element_type=f32)
    grad_attended = jnp.einsum(
        "te,de->td", branch_rows, out_full, preferred_element_type=f32
    ).astype(bf16)
    grad_query, grad_key, grad_value = lax.map(
        attend_back,
        (
            query_seq,
            all_keys,
            all_values,
            grad_attended.reshape(groups, local_len, KV_HEADS, repeats, HEAD_DIM),
            logsum,
            own_positions,
            positions,
        ),
    )
    kv_grad = jnp.concatenate(
        [
            grad_key.reshape(groups, SEQ_LEN, kv_width),
            grad_value.reshape(groups, SEQ_LEN, kv_width),
        ],
        axis=-1,
    )
    own_kv = core_order(
        kv_grad.reshape(groups, ctx_count, local_len, 2 * kv_width).transpose(1, 0, 2, 3)
    )
    for step in ctx_steps():
        own_kv = halve(own_kv, step)
    own_kv = own_kv.reshape(row_count, 2 * kv_width)
    query_back = rotate_back(
        grad_query.reshape(row_count, KV_HEADS, repeats, HEAD_DIM),
        cosine[:, None, None, :],
        sine[:, None, None, :],
    ).reshape(row_count, model_width)
    key_back = rotate_back(
        own_kv[:, :kv_width].reshape(row_count, KV_HEADS, HEAD_DIM),
        cosine[:, None, :],
        sine[:, None, :],
    ).reshape(row_count, kv_width)
    grad_proj = jnp.concatenate([query_back, key_back, own_kv[:, kv_width:]], axis=-1).astype(bf16)
    grad_qkv = jnp.einsum("td,te->de", normed_one, grad_proj, preferred_element_type=f32)
    grad_qkv, pair = lax.optimization_barrier((grad_qkv, pair))
    pair = lax.all_to_all(pair, "ctx", split_axis=0, concat_axis=0, tiled=True)
    pair = pair_join(pair)
    pair = (
        pair.reshape(replica_count, ctx_count, 2, own_rows, shard_count, half_ff)
        .transpose(2, 3, 1, 4, 0, 5)
        .reshape(2, own_rows, ff_width)
        .astype(f32)
    )
    grad_bias = jnp.sum(grad_proj, axis=0, dtype=f32)
    grad_norm_one = jnp.einsum("te,de->td", grad_proj, qkv_full, preferred_element_type=f32)
    gain_one, grad_first = norm_back(resid, first_inv, gain_rows[0], grad_norm_one)
    input_grad = (grad_middle + grad_first).reshape(groups, local_len, model_width)
    own_gains = jnp.stack([gain_one, gain_two]).reshape(2, -1, own_rows).transpose(1, 0, 2)
    small = jnp.concatenate(
        [grad_bias.reshape(-1, bias_len), own_gains.reshape(-1, 2 * own_rows)], axis=1
    )
    name, pairs, _ = axis_steps("replica")[0]
    small = small + lax.ppermute(small, name, pairs)
    small = core_order(small.reshape(ctx_count, shard_count, -1))
    for step in ctx_steps():
        small = halve(small, step)
    small = small[0]
    for step in axis_steps("shard"):
        small = halve(small, step)
    bias_sum = small[0, :bias_len]
    gain_sum = small[0, bias_len:].reshape(2, own_rows)
    return (
        block_out,
        input_grad,
        owner_sum(grad_qkv),
        bias_sum,
        owner_sum(grad_out),
        gain_sum,
        pair[0],
        pair[1],
        grad_down,
    )


def solution(mesh):
    placed = (
        P(("shard", "replica"), "ctx", None),
        P(("shard", "replica"), None),
        P(("ctx", "shard"), None),
        P(("ctx", "shard")),
        P(("ctx", "shard"), None),
        P(None, ("ctx", "shard")),
        P(("ctx", "shard"), None),
        P(("ctx", "shard"), None),
        P(("ctx", "shard"), None),
        P(("shard", "replica"), "ctx", None),
    )
    return jax.shard_map(
        local,
        mesh=mesh,
        in_specs=placed,
        out_specs=(
            P(("shard", "replica"), "ctx", None),
            P(("shard", "replica"), "ctx", None),
            P(("ctx", "shard"), None),
            P(("ctx", "shard")),
            P(("ctx", "shard"), None),
            P(None, ("ctx", "shard")),
            P(("ctx", "shard"), None),
            P(("ctx", "shard"), None),
            P(("ctx", "shard"), None),
        ),
        check_vma=False,
    )
```

```python
import jax
import jax.numpy as jnp
from jax import lax
from jax.sharding import PartitionSpec as P

Q_HEADS = 14
KV_HEADS = 2
HEAD_DIM = 64
SEQ_LEN = 1024


epsilon = 1e-06
rope_base = 1000000.0
score_scale = 0.125
masked_value = -1e30


def rope_tables(positions):
    half_dim = HEAD_DIM // 2
    inverse = rope_base ** (-(jnp.arange(half_dim, dtype=jnp.float32) * 2.0) / HEAD_DIM)
    angles = positions.astype(jnp.float32)[..., None] * inverse
    angles = jnp.concatenate([angles, angles], axis=-1)
    return (jnp.cos(angles), jnp.sin(angles))


def rotate(values, cosine, sine):
    half_dim = values.shape[-1] // 2
    turned = jnp.concatenate([-values[..., half_dim:], values[..., :half_dim]], axis=-1)
    return values * cosine + turned * sine


def rotate_back(grads, cosine, sine):
    half_dim = grads.shape[-1] // 2
    moved = grads * sine
    turned = jnp.concatenate([moved[..., half_dim:], -moved[..., :half_dim]], axis=-1)
    return grads * cosine + turned


def norm_back(inputs, inverse, gain, upstream):
    scaled = upstream * gain
    gain_term = jnp.sum(upstream * inputs * inverse, axis=0)
    input_term = inverse * scaled - inputs * inverse**3 * jnp.mean(
        scaled * inputs, axis=-1, keepdims=True
    )
    return (gain_term, input_term)


def masked_scores(queries, key_rows, pos_query, pos_key):
    scores = (
        jnp.einsum("qhrd,khd->hrqk", queries, key_rows, preferred_element_type=jnp.float32)
        * score_scale
    )
    allowed = pos_query[:, None] >= pos_key[None, :]
    return jnp.where(allowed, scores, masked_value)


def attend(packed):
    queries, key_rows, value_rows, pos_query, pos_key = packed
    scores = masked_scores(queries, key_rows, pos_query, pos_key)
    top_score = jnp.max(scores, axis=-1, keepdims=True)
    weights = jnp.exp(scores - top_score)
    totals = jnp.sum(weights, axis=-1, keepdims=True)
    attn_probs = (weights / totals).astype(jnp.bfloat16)
    mixed_out = jnp.einsum(
        "hrqk,khd->qhrd", attn_probs, value_rows, preferred_element_type=jnp.float32
    )
    return (mixed_out, top_score + jnp.log(totals))


def attend_back(packed):
    queries, key_rows, value_rows, upstream, logsum, pos_query, pos_key = packed
    scores = masked_scores(queries, key_rows, pos_query, pos_key)
    attn_probs = jnp.exp(scores - logsum)
    dprob = jnp.einsum("qhrd,khd->hrqk", upstream, value_rows, preferred_element_type=jnp.float32)
    row_dot = jnp.sum(attn_probs * dprob, axis=-1, keepdims=True)
    dscore = (attn_probs * (dprob - row_dot)).astype(jnp.bfloat16)
    grad_query = (
        jnp.einsum("hrqk,khd->qhrd", dscore, key_rows, preferred_element_type=jnp.float32)
        * score_scale
    )
    grad_key = (
        jnp.einsum("hrqk,qhrd->khd", dscore, queries, preferred_element_type=jnp.float32)
        * score_scale
    )
    grad_value = jnp.einsum(
        "hrqk,qhrd->khd",
        attn_probs.astype(jnp.bfloat16),
        upstream,
        preferred_element_type=jnp.float32,
    )
    return (grad_query, grad_key, grad_value)


def reverse_bits(value, count):
    return sum(((value >> at) & 1) << (count - 1 - at) for at in range(count))


def ctx_steps():
    count = lax.axis_size("ctx").bit_length() - 1
    replica = lax.axis_index("replica")
    index = lax.axis_index("ctx")
    index = jnp.where(replica == 0, index, reverse_bits(index, count))
    steps = []
    for at in reversed(range(count)):
        masks = (1 << at, 1 << (count - 1 - at))
        pairs = [
            (ctx * 2 + core, (ctx ^ masks[core]) * 2 + core)
            for ctx in range(1 << count)
            for core in range(2)
        ]
        steps.append((("ctx", "replica"), pairs, (index >> at) & 1))
    return steps


def axis_steps(name):
    size = lax.axis_size(name)
    index = lax.axis_index(name)
    return [
        (name, [(own, own ^ (1 << at)) for own in range(size)], (index >> at) & 1)
        for at in reversed(range(size.bit_length() - 1))
    ]


def core_order(parts):
    count = parts.shape[0].bit_length() - 1
    rest = parts.shape[1:]
    dims = tuple(reversed(range(count))) + tuple(range(count, count + len(rest)))
    turned = parts.reshape((2,) * count + rest).transpose(dims).reshape(parts.shape)
    return jnp.where(lax.axis_index("replica") == 0, parts, turned)


def halve(parts, step):
    names, pairs, bit = step
    split = parts.reshape((2, parts.shape[0] // 2) + parts.shape[1:])
    kept = lax.dynamic_index_in_dim(split, bit, 0, keepdims=False)
    sent = lax.dynamic_index_in_dim(split, 1 - bit, 0, keepdims=False)
    arrived = lax.ppermute(sent.astype(jnp.bfloat16), names, pairs)
    return kept.astype(jnp.float32) + arrived.astype(jnp.float32)


def double(parts, step):
    names, pairs, bit = step
    other = lax.ppermute(parts, names, pairs)
    return jnp.concatenate([jnp.where(bit == 0, parts, other), jnp.where(bit == 0, other, parts)])


def gather_shards(own):
    steps = axis_steps("shard")
    parts = own.reshape((1,) * len(steps) + own.shape)
    for at, (name, pairs, bit) in enumerate(steps):
        other = lax.ppermute(parts, name, pairs)
        parts = jnp.concatenate(
            [jnp.where(bit == 0, parts, other), jnp.where(bit == 0, other, parts)], axis=at
        )
    return parts.reshape((-1,) + own.shape[1:])


def scatter_shards(rows):
    steps = axis_steps("shard")
    parts = rows.reshape((2,) * len(steps) + (-1,) + rows.shape[1:])
    for at, (name, pairs, bit) in reversed(list(enumerate(steps))):
        kept = lax.dynamic_index_in_dim(parts, bit, at, keepdims=False)
        sent = lax.dynamic_index_in_dim(parts, 1 - bit, at, keepdims=False)
        arrived = lax.ppermute(sent.astype(jnp.bfloat16), name, pairs)
        parts = kept.astype(jnp.float32) + arrived.astype(jnp.float32)
    return parts


def pair_join(values):
    return double(values[None], axis_steps("replica")[0])


def gather_group(rows):
    for names, pairs, _ in ctx_steps() + axis_steps("replica"):
        rows = jnp.concatenate([rows, lax.ppermute(rows, names, pairs)])
    return rows


def scatter_group(rows):
    for names, pairs, _ in reversed(ctx_steps() + axis_steps("replica")):
        half = rows.shape[0] // 2
        arrived = lax.ppermute(rows[half:].astype(jnp.bfloat16), names, pairs)
        rows = rows[:half] + arrived.astype(jnp.float32)
    return rows


def gather_owners(own, beside=None):
    rows, width = own.shape
    halves = own.reshape(rows, 2, width // 2)
    parts = lax.dynamic_index_in_dim(halves, lax.axis_index("replica"), 1, keepdims=False)[None]
    for step in reversed(axis_steps("shard")):
        parts = double(parts, step)
    if beside is not None:
        parts, beside = lax.optimization_barrier((parts, beside))
    parts = parts[None]
    for step in reversed(ctx_steps()):
        parts = double(parts, step)
    parts = core_order(parts)
    both = pair_join(parts.reshape(-1, width // 2))
    return jnp.concatenate([both[0], both[1]], axis=1), beside


def owner_sum(grad):
    rows, width = grad.shape
    ctx_count = lax.axis_size("ctx")
    shard_count = lax.axis_size("shard")
    halves = grad.reshape(rows, 2, width // 2).transpose(1, 0, 2)
    parts = halve(halves, axis_steps("replica")[0])
    parts = core_order(parts.reshape(ctx_count, shard_count, -1, width // 2))
    for step in ctx_steps():
        parts = halve(parts, step)
    parts = parts[0]
    for step in axis_steps("shard"):
        parts = halve(parts, step)
    both = pair_join(parts[0].astype(jnp.bfloat16))
    return jnp.concatenate([both[0], both[1]], axis=1).astype(jnp.float32)


def local(tokens, block_order, w_qkv, qkv_bias, w_out, norm_gains, w_gate, w_up, w_down, cotangent):
    groups, local_len, model_width = tokens.shape
    kv_width = KV_HEADS * HEAD_DIM
    repeats = Q_HEADS // KV_HEADS
    ctx_count = lax.axis_size("ctx")
    shard_count = lax.axis_size("shard")
    replica_count = lax.axis_size("replica")
    ctx_index = lax.axis_index("ctx")
    replica_index = lax.axis_index("replica")
    block_len = local_len // 2
    row_count = groups * local_len
    own_rows, ff_width = w_gate.shape
    own_ff = w_down.shape[0]
    half_ff = own_ff // replica_count
    slice_ff = shard_count * half_ff
    qkv_width = w_qkv.shape[1]
    f32, bf16 = jnp.float32, jnp.bfloat16

    slots = jnp.arange(SEQ_LEN, dtype=jnp.int32)
    owners = (
        (slots // block_len)[:, None] == jnp.arange(2 * ctx_count, dtype=jnp.int32)[None, :]
    ).astype(jnp.int32)
    positions = (
        jnp.sum(block_order[:, None, :] * owners[None], axis=-1) * block_len + slots % block_len
    )
    own_positions = lax.dynamic_slice_in_dim(positions, ctx_index * local_len, local_len, 1)

    def unit_slice(weight):
        own = lax.dynamic_index_in_dim(
            weight.reshape(own_rows, ctx_count, shard_count, replica_count, half_ff),
            replica_index,
            3,
            keepdims=False,
        )
        return own.reshape(own_rows, ctx_count, slice_ff).transpose(1, 0, 2)

    gate_up = jnp.stack([unit_slice(w_gate), unit_slice(w_up)], axis=1)
    gate_up = lax.all_to_all(gate_up, "ctx", split_axis=0, concat_axis=0, tiled=True)
    qkv_full, gate_up = gather_owners(w_qkv, gate_up)
    bias_len = qkv_bias.shape[0]
    extras = jnp.concatenate([qkv_bias, norm_gains.reshape(-1)])[None]
    for step in reversed(axis_steps("shard")):
        extras = double(extras, step)
    extras = extras[None]
    for step in reversed(ctx_steps()):
        extras = double(extras, step)
    extras = core_order(extras).reshape(ctx_count * shard_count, -1)
    bias_full = extras[:, :bias_len].reshape(-1)
    gains_full = (
        extras[:, bias_len:].reshape(-1, 2, own_rows).transpose(1, 0, 2).reshape(2, model_width)
    )
    qkv_full, w_out, w_down, cotangent = lax.optimization_barrier(
        (qkv_full, w_out, w_down, cotangent)
    )
    out_full, _ = gather_owners(w_out)

    gate_up = lax.all_gather(gate_up, "shard", axis=0, tiled=False)
    gate_up = gate_up.transpose(2, 1, 0, 3, 4).reshape(2, model_width, slice_ff)
    down_part = gather_shards(
        lax.dynamic_slice_in_dim(w_down, replica_index * half_ff, half_ff, 0)
    )
    grad_top = cotangent.reshape(row_count, model_width)
    top_all = gather_group(grad_top)

    gain_rows = gains_full.astype(f32)
    resid = tokens.reshape(row_count, model_width).astype(f32)
    first_inv = lax.rsqrt(jnp.mean(resid * resid, axis=-1, keepdims=True) + epsilon)
    normed_one = (resid * first_inv * gain_rows[0]).astype(bf16)
    projected = jnp.dot(normed_one, qkv_full, preferred_element_type=f32) + bias_full.astype(f32)
    cosine, sine = rope_tables(own_positions.reshape(row_count))
    query_rows = rotate(
        projected[:, :model_width].reshape(row_count, KV_HEADS, repeats, HEAD_DIM),
        cosine[:, None, None, :],
        sine[:, None, None, :],
    ).astype(bf16)
    key_rows = rotate(
        projected[:, model_width : model_width + kv_width].reshape(row_count, KV_HEADS, HEAD_DIM),
        cosine[:, None, :],
        sine[:, None, :],
    ).astype(bf16)
    value_rows = projected[:, model_width + kv_width :].astype(bf16)
    kv_local = jnp.concatenate([key_rows.reshape(row_count, kv_width), value_rows], axis=-1)
    kv_all = lax.all_gather(
        kv_local.reshape(groups, local_len, 2 * kv_width), "ctx", axis=1, tiled=True
    )
    all_keys = kv_all[..., :kv_width].reshape(groups, SEQ_LEN, KV_HEADS, HEAD_DIM)
    all_values = kv_all[..., kv_width:].reshape(groups, SEQ_LEN, KV_HEADS, HEAD_DIM)
    query_seq = query_rows.reshape(groups, local_len, KV_HEADS, repeats, HEAD_DIM)
    attended, logsum = lax.map(
        attend, (query_seq, all_keys, all_values, own_positions, positions)
    )
    attn_rows = attended.reshape(row_count, model_width).astype(bf16)
    middle = resid + jnp.dot(attn_rows, out_full, preferred_element_type=f32)
    middle, gate_up = lax.optimization_barrier((middle, gate_up))
    gate_part, up_part = gate_up[0], gate_up[1]
    second_inv = lax.rsqrt(jnp.mean(middle * middle, axis=-1, keepdims=True) + epsilon)
    normed_two = (middle * second_inv * gain_rows[1]).astype(bf16)

    normed_all = gather_group(normed_two)
    gate_pre = jnp.dot(normed_all, gate_part, preferred_element_type=f32)
    up_pre = jnp.dot(normed_all, up_part, preferred_element_type=f32)
    grad_act = jnp.einsum("td,fd->tf", top_all, down_part, preferred_element_type=f32)
    sigmoid_gate = jax.nn.sigmoid(gate_pre)
    act_rows = (gate_pre * sigmoid_gate * up_pre).astype(bf16)
    grad_gate_rows = (
        grad_act * up_pre * sigmoid_gate * (1.0 + gate_pre * (1.0 - sigmoid_gate))
    ).astype(bf16)
    grad_up_rows = (grad_act * gate_pre * sigmoid_gate).astype(bf16)
    norm_part = jnp.einsum(
        "tf,df->td", grad_gate_rows, gate_part, preferred_element_type=f32
    ) + jnp.einsum("tf,df->td", grad_up_rows, up_part, preferred_element_type=f32)
    grad_norm_two = scatter_group(norm_part)
    out_part = jnp.dot(act_rows, down_part, preferred_element_type=f32)
    grad_down = jnp.einsum("tf,td->fd", act_rows, top_all, preferred_element_type=f32)
    out_part, grad_down, grad_norm_two = lax.optimization_barrier(
        (out_part, grad_down, grad_norm_two)
    )
    out_sum = scatter_group(out_part)
    down_sum = scatter_shards(grad_down).astype(bf16)
    grad_gate = jnp.einsum("td,tf->df", normed_all, grad_gate_rows, preferred_element_type=f32)
    grad_up = jnp.einsum("td,tf->df", normed_all, grad_up_rows, preferred_element_type=f32)
    pair = jnp.stack(
        [
            grad_gate.astype(bf16).reshape(ctx_count, shard_count, own_rows, slice_ff),
            grad_up.astype(bf16).reshape(ctx_count, shard_count, own_rows, slice_ff),
        ]
    ).transpose(2, 1, 0, 3, 4)
    pair = lax.psum_scatter(
        pair.reshape(-1, slice_ff), "shard", scatter_dimension=0, tiled=True
    ).reshape(ctx_count, 2, own_rows, slice_ff)
    gain_two, grad_middle = norm_back(middle, second_inv, gain_rows[1], grad_norm_two)
    grad_middle = grad_middle + grad_top.astype(f32)
    branch_rows = grad_middle.astype(bf16)
    grad_out = jnp.einsum("td,te->de", attn_rows, branch_rows, preferred_element_type=f32)
    grad_attended = jnp.einsum(
        "te,de->td", branch_rows, out_full, preferred_element_type=f32
    ).astype(bf16)
    grad_query, grad_key, grad_value = lax.map(
        attend_back,
        (
            query_seq,
            all_keys,
            all_values,
            grad_attended.reshape(groups, local_len, KV_HEADS, repeats, HEAD_DIM),
            logsum,
            own_positions,
            positions,
        ),
    )
    kv_grad = jnp.concatenate(
        [
            grad_key.reshape(groups, SEQ_LEN, kv_width),
            grad_value.reshape(groups, SEQ_LEN, kv_width),
        ],
        axis=-1,
    )
    own_kv = core_order(
        kv_grad.reshape(groups, ctx_count, local_len, 2 * kv_width).transpose(1, 0, 2, 3)
    )
    for step in ctx_steps():
        own_kv = halve(own_kv, step)
    own_kv, pair, out_sum, down_sum = lax.optimization_barrier((own_kv, pair, out_sum, down_sum))
    block_out = (middle + out_sum).astype(bf16).reshape(groups, local_len, model_width)
    grad_down = pair_join(down_sum).reshape(own_ff, model_width).astype(f32)
    pair = lax.all_to_all(pair, "ctx", split_axis=0, concat_axis=0, tiled=True)
    pair = pair_join(pair)
    pair = (
        pair.reshape(replica_count, ctx_count, 2, own_rows, shard_count, half_ff)
        .transpose(2, 3, 1, 4, 0, 5)
        .reshape(2, own_rows, ff_width)
        .astype(f32)
    )
    own_kv = own_kv.reshape(row_count, 2 * kv_width)
    query_back = rotate_back(
        grad_query.reshape(row_count, KV_HEADS, repeats, HEAD_DIM),
        cosine[:, None, None, :],
        sine[:, None, None, :],
    ).reshape(row_count, model_width)
    key_back = rotate_back(
        own_kv[:, :kv_width].reshape(row_count, KV_HEADS, HEAD_DIM),
        cosine[:, None, :],
        sine[:, None, :],
    ).reshape(row_count, kv_width)
    grad_proj = jnp.concatenate([query_back, key_back, own_kv[:, kv_width:]], axis=-1).astype(bf16)
    grad_qkv = jnp.einsum("td,te->de", normed_one, grad_proj, preferred_element_type=f32)
    grad_bias = jnp.sum(grad_proj, axis=0, dtype=f32)
    grad_norm_one = jnp.einsum("te,de->td", grad_proj, qkv_full, preferred_element_type=f32)
    gain_one, grad_first = norm_back(resid, first_inv, gain_rows[0], grad_norm_one)
    input_grad = (grad_middle + grad_first).reshape(groups, local_len, model_width)
    own_gains = jnp.stack([gain_one, gain_two]).reshape(2, -1, own_rows).transpose(1, 0, 2)
    small = jnp.concatenate(
        [grad_bias.reshape(-1, bias_len), own_gains.reshape(-1, 2 * own_rows)], axis=1
    )
    name, pairs, _ = axis_steps("replica")[0]
    small = small + lax.ppermute(small, name, pairs)
    small = core_order(small.reshape(ctx_count, shard_count, -1))
    for step in ctx_steps():
        small = halve(small, step)
    small = small[0]
    for step in axis_steps("shard"):
        small = halve(small, step)
    bias_sum = small[0, :bias_len]
    gain_sum = small[0, bias_len:].reshape(2, own_rows)
    return (
        block_out,
        input_grad,
        owner_sum(grad_qkv),
        bias_sum,
        owner_sum(grad_out),
        gain_sum,
        pair[0],
        pair[1],
        grad_down,
    )


def solution(mesh):
    placed = (
        P(("shard", "replica"), "ctx", None),
        P(("shard", "replica"), None),
        P(("ctx", "shard"), None),
        P(("ctx", "shard")),
        P(("ctx", "shard"), None),
        P(None, ("ctx", "shard")),
        P(("ctx", "shard"), None),
        P(("ctx", "shard"), None),
        P(("ctx", "shard"), None),
        P(("shard", "replica"), "ctx", None),
    )
    return jax.shard_map(
        local,
        mesh=mesh,
        in_specs=placed,
        out_specs=(
            P(("shard", "replica"), "ctx", None),
            P(("shard", "replica"), "ctx", None),
            P(("ctx", "shard"), None),
            P(("ctx", "shard")),
            P(("ctx", "shard"), None),
            P(None, ("ctx", "shard")),
            P(("ctx", "shard"), None),
            P(("ctx", "shard"), None),
            P(("ctx", "shard"), None),
        ),
        check_vma=False,
    )
```
